32 devices in a mesh: groups: 2 (over x), col: 16 (over z, y, core).
Axes of the slice: x: 2, y: 2, z: 4, core: 2. Of those that a mesh axis runs over, the one named last changes fastest.
Arguments:
- features: bfloat16 [8192, 256], P(('groups', 'col')), parts along dimension 0, may hold values from -6 to 6
- block_values: bfloat16 [4096, 128, 128], P(('groups', 'col')), parts along dimension 0, may hold values from -0.09375 to 0.09375
- block_owner: int32 [4096, 1], P(('groups', 'col')), parts along dimension 0, may hold values from 0 to 15; in each aligned block of 128 rows (0 to 127, 128 to 255, ...) at most 16 rows name the same one
- block_sub: int32 [4096], P(('groups', 'col')), parts along dimension 0, may hold values from 0 to 1
- block_col: int32 [4096], P(('groups', 'col')), parts along dimension 0, may hold values from 0 to 1
- block_valid: int32 [4096], P(('groups', 'col')), parts along dimension 0, may hold values from 0 to 1, as said below
- norm_gain: float32 [256], replicated, may hold values from 0.1 to 1.9
- weight: bfloat16 [256, 256], replicated, may hold values from -0.375 to 0.375
Outputs:
- propagated: float32 [8192, 256], P(('groups', 'col')), parts along dimension 0
The draws below stay inside these ranges and needn't reach their ends.
There are 2 independent parts, one for each index of `groups`. The reference program is written for one: setup_inputs(seed, part) draws one part's arguments, and reference() takes and returns one part's arrays. A program takes and returns all parts, laid end to end along the dimension named above; an argument that names none is the same for every part. Nothing has to cross between parts.
Inputs may be any that keep to these rules, and one draw needn't show every extreme that they name: `block_owner`: in the 128 slots of one tile no owner is named more than 16 times; in every draw some owner is named exactly 16 times in some tile. `block_valid`: each tile has at least 16 live slots, and in every draw some tile has all 128 slots live.
All inputs are finite; a program needn't handle non-finite values.
Results may differ from the reference program's by a relative error of at most 0.0032.
Values may be sent and summed in bfloat16 or wider, within the bound.
A program may use at most 128 MiB of HBM per device.

```python
import math
import jax
import jax.numpy as jnp
import numpy as np
from jax import lax

F = 256
BS = 128
NODE_DEV = 256
NB = 128
NODES = 4096
NBT = 2048
MOST = 16
N_COL = 16


def draw_block_valid(key, part):
    key = jax.random.fold_in(key, 7)
    key_count, key_full, key_order = jax.random.split(key, 3)
    counts = jax.random.randint(key_count, (N_COL,), NB // 8, NB + 1)
    full_tile = jax.random.randint(key_full, (), 0, N_COL)
    counts = jnp.where(jnp.arange(N_COL) == full_tile, NB, counts)
    orders = jax.vmap(lambda single: jax.random.permutation(single, NB))(jax.random.split(key_order, N_COL))
    return (orders < counts[:, None]).astype(jnp.int32).reshape(N_COL * NB)


def touch_ends(result, key, low, largest):
    spot = [jax.random.randint(jax.random.fold_in(key, axis), (), 0, length) for axis, length in enumerate(result.shape)]
    widest = result.shape.index(max(result.shape))
    beside = spot[:widest] + [(spot[widest] + 1) % result.shape[widest]] + spot[widest + 1:]
    return result.at[tuple(spot)].set(low).at[tuple(beside)].set(largest)


def shard_levels(own_key, dims, cuts, low, top_value):
    def one(position, shards_of):
        draws = jax.random.uniform(jax.random.fold_in(jax.random.fold_in(own_key, 6), position), (shards_of,), jnp.float32, low / len(cuts), top_value / len(cuts))
        return jnp.repeat(jnp.exp(draws), dims[position] // shards_of).reshape((-1,) + (1,) * (len(dims) - position - 1))

    loudness = one(*cuts[0])
    for cut in cuts[1:]:
        loudness = loudness * one(*cut)
    return loudness


def routed_block(stream_key, own, number, rows, count, top, reach, skew):
    ranking = jax.random.permutation(stream_key, count)
    heavy_load, usual = load_shares(count, rows * top, reach, skew, True), load_shares(count, rows * top, reach, skew, False)
    places = jnp.arange(count)

    def named(lengths, offset_by):
        used = int((lengths > 0).sum())
        fixed = max(1, used // 4)
        shifted = fixed + (places - fixed + offset_by * (used - fixed)) % max(1, count - fixed)
        return jnp.zeros((count,), jnp.int32).at[ranking[jnp.where(places < fixed, places, shifted)]].set(jnp.asarray(lengths, jnp.int32))

    lengths = jnp.where(number % 4 == 0, named(heavy_load, number // 4), named(usual, number - number // 4 - 1))
    mixed = jax.random.permutation(jax.random.fold_in(own, 3), count)
    giver, taker = mixed[0:count // 2 * 2:2], mixed[1:count // 2 * 2:2]
    margin = jnp.minimum(lengths[giver] - 1, reach - lengths[taker]) // 2
    margin = jnp.where((giver == ranking[0]) | (taker == ranking[0]) | (lengths[taker] == 0), 0, jnp.maximum(margin, 0))
    shifted = jax.random.randint(jax.random.fold_in(own, 4), (count // 2,), 0, 1 << 20) % (margin + 1)
    lengths = lengths.at[giver].add(-shifted).at[taker].add(shifted)
    members = jnp.searchsorted(jnp.cumsum(lengths), jnp.arange(rows * top), side="right").astype(jnp.int32)
    listing = members.reshape(top, rows).T
    listing = listing[jax.random.permutation(jax.random.fold_in(own, 1), rows)]
    offset_by = jax.random.randint(jax.random.fold_in(own, 2), (rows, 1), 0, top)
    return jnp.take_along_axis(listing, (jnp.arange(top)[None, :] + offset_by) % top, axis=1)


def load_shares(amount, total, bound, slope, full):
    loads = [(1 << 20) // math.isqrt(rank ** slope) + 1 for rank in range(1, amount + 1)]
    largest = bound if full else min(bound, max(-(-total // amount), total * loads[0] // sum(loads)))
    least = 1 if total - largest >= amount - 1 else 0
    holding, spare = [largest] + [least] * (amount - 1), total - largest - least * (amount - 1)
    while spare > 0:
        free = [i for i in range(1, amount) if holding[i] < largest] or [i for i in range(1, amount) if holding[i] < bound]
        whole, remaining = sum([loads[i] for i in free]), spare
        for i in free:
            extra = min(bound - holding[i], max(1, remaining * loads[i] // whole), spare)
            holding[i] = holding[i] + extra
            spare = spare - extra
    return np.array(holding)


def centred(key, shape, scale, bound, cuts=(), dtype=jnp.bfloat16):
    values = scale * jax.random.normal(key, shape, jnp.float32)
    if cuts:
        values = values * shard_levels(key, shape, cuts, -0.22, 0.18)
    return jnp.clip(values, -bound, bound).astype(dtype)


def setup_inputs(seed: int = 0, part: int = 0) -> dict:
    key_of = jax.random.split(jax.random.key(seed), 9)
    part_keys = jax.random.split(jax.random.fold_in(key_of[8], part), 9)
    features = centred(part_keys[0], (NODES, F), 1.0, 6.0, ((0, 16),))
    block_values = centred(part_keys[1], (NBT, BS, BS), (BS * NB * BS // NODE_DEV // 2) ** -0.5, 0.09375, ((0, 16),))
    block_owner_keys = jax.random.split(jax.random.fold_in(part_keys[2], 1), NBT // NB)
    block_owner_turns = jax.random.permutation(jax.random.fold_in(part_keys[2], 3), NBT // NB)
    block_owner = jax.vmap(lambda own, number: routed_block(jax.random.fold_in(part_keys[2], 2), own, number, NB, N_COL, 1, MOST, 2))(block_owner_keys, block_owner_turns).reshape((NBT, 1))
    block_sub = touch_ends(jax.random.randint(part_keys[3], (NBT,), 0, NODE_DEV // BS), jax.random.fold_in(part_keys[3], 1), 0, (NODE_DEV // BS) - 1).astype(jnp.int32)
    block_col = touch_ends(jax.random.randint(part_keys[4], (NBT,), 0, NODE_DEV // BS), jax.random.fold_in(part_keys[4], 1), 0, (NODE_DEV // BS) - 1).astype(jnp.int32)
    block_valid = draw_block_valid(jax.random.fold_in(jax.random.fold_in(key_of[8], part), 71), part)
    norm_gain = jnp.clip(1.0 + 0.18 * jax.random.normal(key_of[6], (F,), jnp.float32), 0.1, 1.9)
    weight = centred(key_of[7], (F, F), F ** -0.5, 0.375)
    return dict(features=features, block_values=block_values, block_owner=block_owner, block_sub=block_sub, block_col=block_col, block_valid=block_valid, norm_gain=norm_gain, weight=weight)


def reference(features, block_values, block_owner, block_sub, block_col, block_valid, norm_gain, weight):
    per_dev = NODE_DEV // BS
    total_blocks = NODES // BS
    tile_rows = (block_owner[:, 0] * per_dev + block_sub).reshape(N_COL, NB)
    tile_cols = block_col.reshape(N_COL, NB)
    tile_mask = block_valid.reshape(N_COL, NB).astype(jnp.float32)
    tile_values = block_values.reshape(N_COL, NB, BS, BS)
    tile_source = features.reshape(N_COL, per_dev, BS, F)

    def forward(running, tile_data):
        values, rows_here, cols_here, mask_here, source = tile_data
        picked = source[cols_here].astype(jnp.float32)
        products = jnp.einsum('sab,sbf->saf', values.astype(jnp.float32), picked) * mask_here[:, None, None]
        return (running + jax.ops.segment_sum(products, rows_here, num_segments=total_blocks), None)
    start_sum = jnp.zeros((total_blocks, BS, F), jnp.float32)
    aggregate, _ = lax.scan(forward, start_sum, (tile_values, tile_rows, tile_cols, tile_mask, tile_source))
    aggregate = aggregate.reshape(NODES, F)
    row_scale = lax.rsqrt(lax.optimization_barrier(jnp.mean(aggregate * aggregate, axis=1)) + 1e-06)
    normed = (aggregate * row_scale[:, None] * norm_gain[None, :]).astype(jnp.bfloat16)
    hidden = jax.nn.relu(jnp.dot(normed, weight, preferred_element_type=jnp.float32)).astype(jnp.bfloat16)
    hidden_blocks = hidden.reshape(total_blocks, BS, F)

    def backward(carried, tile_data):
        values, rows_here, cols_here, mask_here = tile_data
        picked = hidden_blocks[rows_here].astype(jnp.float32)
        returned = jnp.einsum('sab,saf->sbf', values.astype(jnp.float32), picked) * mask_here[:, None, None]
        return (carried, jax.ops.segment_sum(returned, cols_here, num_segments=per_dev))
    _, result_rows = lax.scan(backward, jnp.zeros((), jnp.float32), (tile_values, tile_rows, tile_cols, tile_mask))
    return result_rows.reshape(NODES, F)
```

```python
import functools

import jax
import jax.numpy as jnp
from jax import lax
from jax.experimental import pallas as pl
from jax.experimental.pallas import tpu as pltpu
from jax.sharding import PartitionSpec as P

MIB = 1024 * 1024
CHUNKS = 8


def merge_kernel(n, bs, nb, owner_ref, sub_ref, col_ref, valid_ref, values_ref, hi_ref, lo_ref,
                 dense, staged, sems):
    zs = n // 4
    per = nb // CHUNKS

    def chunk(i):
        part = pl.ds(i * per, per)
        return pltpu.make_async_copy(values_ref.at[part], staged.at[part], sems.at[i])

    for i in range(CHUNKS):
        chunk(i).start()

    @pl.loop(0, n)
    def _(d):
        dense[d] = jnp.zeros(dense.shape[1:], jnp.float32)

    for i in range(CHUNKS):
        chunk(i).wait()

        @pl.loop(i * per, (i + 1) * per)
        def _(s):
            owner = owner_ref[s]
            place = (owner % 2 * 2 + owner // 2 % 2) * zs + owner // 4
            rows = pl.ds(pl.multiple_of(sub_ref[s] * bs, bs), bs)
            columns = pl.ds(pl.multiple_of(col_ref[s] * bs, bs), bs)
            live = valid_ref[s].astype(jnp.float32)
            dense[place, rows, columns] += staged[s].astype(jnp.float32) * live

    @pl.loop(0, n)
    def _(d):
        whole = dense[d]
        head = whole.astype(jnp.bfloat16)
        hi_ref[d] = head
        lo_ref[d] = (whole - head.astype(jnp.float32)).astype(jnp.bfloat16)


def layer_kernel(n, hi_ref, lo_ref, x_ref, gain_ref, w_ref, out_ref,
                 pa_send, pa_recv, yb_send, yb_recv, zb_send, zb_recv, acc, agg, hbuf, out_t,
                 pa_ss, pa_rs, yb_ss, yb_rs, zb_ss, zb_rs, hz_ss, hz_rs, hy_ss, hy_rs, hc_ss, hc_rs):
    zs = n // 4
    me = lax.axis_index("col")
    z, y, c = me // 4, me // 2 % 2, me % 2
    other_core = me + 1 - 2 * c
    other_y = me + 2 - 4 * y

    def dest(z_to):
        return z_to * 4 + y * 2 + c

    barrier = pltpu.get_barrier_semaphore()

    def greet(device):
        pl.semaphore_signal(barrier, inc=1, device_id={"col": device},
                            device_id_type=pl.DeviceIdType.MESH)

    greet(other_core)
    greet(other_y)
    for i in range(1, zs):
        greet(dest((z + i) % zs))
    pl.semaphore_wait(barrier, zs + 1)

    def remote(src, dst, ss, rs, device):
        return pltpu.make_async_remote_copy(
            src_ref=src, dst_ref=dst, send_sem=ss, recv_sem=rs,
            device_id={"col": device}, device_id_type=pl.DeviceIdType.MESH)

    def product(place):
        x = x_ref[...]
        return (jnp.dot(hi_ref[place], x, preferred_element_type=jnp.float32)
                + jnp.dot(lo_ref[place], x, preferred_element_type=jnp.float32))

    def core_copy(j):
        return remote(pa_send.at[j], pa_recv.at[j], pa_ss.at[j], pa_rs.at[j], other_core)

    def turned(k):
        return (k + (1 - y) * zs) % (2 * zs)

    @pl.loop(0, 2 * zs)
    def _(k):
        j = turned(k)
        pa_send[j] = product((1 - c) * 2 * zs + j)
        core_copy(j).start()

    @pl.loop(0, 2 * zs)
    def _(k):
        j = turned(k)
        acc[j] = product(c * 2 * zs + j)

    def y_copy(k):
        return remote(yb_send.at[k], yb_recv.at[k], yb_ss.at[k], yb_rs.at[k], other_y)

    @pl.loop(0, zs)
    def _(k):
        k = (z + 1 + k) % zs
        j = (1 - y) * zs + k
        core_copy(j).wait_recv()
        yb_send[k] = (acc[j] + pa_recv[j]).astype(jnp.bfloat16)
        y_copy(k).start()

    @pl.loop(0, zs)
    def _(k):
        j = y * zs + k
        core_copy(j).wait_recv()
        acc[j] = acc[j] + pa_recv[j]

    def z_copy(i):
        return remote(zb_send.at[i], zb_recv.at[i], zb_ss.at[i], zb_rs.at[i], dest((z + i) % zs))

    @pl.loop(1, zs)
    def _(i):
        k = (z + i) % zs
        y_copy(k).wait_recv()
        zb_send[i] = (acc[y * zs + k] + yb_recv[k].astype(jnp.float32)).astype(jnp.bfloat16)
        z_copy(i).start()

    y_copy(z).wait_recv()
    agg[...] = acc[y * zs + z] + yb_recv[z].astype(jnp.float32)

    @pl.loop(1, zs)
    def _(i):
        z_copy(i).wait_recv()
        agg[...] += zb_recv[i].astype(jnp.float32)

    total = agg[...]
    scale = lax.rsqrt(jnp.mean(total * total, axis=1, keepdims=True) + 1e-06)
    normed = (total * scale * gain_ref[...]).astype(jnp.bfloat16)
    hidden = jnp.maximum(jnp.dot(normed, w_ref[...], preferred_element_type=jnp.float32), 0.0)
    mine = (c * 2 + y) * zs + z
    hbuf[mine] = hidden.T.astype(jnp.bfloat16)

    def hz_copy(i):
        return remote(hbuf.at[mine], hbuf.at[mine], hz_ss.at[i], hz_rs.at[i], dest((z + i) % zs))

    def hz_wait(i):
        slot = (c * 2 + y) * zs + (z - i + zs) % zs
        remote(hbuf.at[slot], hbuf.at[slot], hz_ss.at[i], hz_rs.at[i], other_y).wait_recv()
        return slot

    def hy_copy(i, y_of):
        slot = (c * 2 + y_of) * zs + (z - i + zs) % zs
        return slot, remote(hbuf.at[slot], hbuf.at[slot], hy_ss.at[i], hy_rs.at[i], other_y)

    def hc_copy(i, c_of, y_of):
        slot = (c_of * 2 + y_of) * zs + (z - i + zs) % zs
        k = (y_of + y) % 2 * zs + i
        return slot, remote(hbuf.at[slot], hbuf.at[slot], hc_ss.at[k], hc_rs.at[k], other_core)

    for i in range(1, zs):
        hz_copy(i).start()

    hy_copy(0, y)[1].start()
    hc_copy(0, c, y)[1].start()
    out_t[...] = jnp.zeros(out_t.shape, jnp.float32)

    def take(slot):
        out_t[...] += (jnp.dot(hbuf[slot], hi_ref[slot], preferred_element_type=jnp.float32)
                       + jnp.dot(hbuf[slot], lo_ref[slot], preferred_element_type=jnp.float32))

    take(mine)

    @pl.loop(1, zs)
    def _(i):
        slot = hz_wait(i)
        hy_copy(i, y)[1].start()
        hc_copy(i, c, y)[1].start()
        take(slot)

    @pl.loop(0, zs)
    def _(i):
        slot, copy = hy_copy(i, 1 - y)
        copy.wait_recv()
        hc_copy(i, c, 1 - y)[1].start()
        take(slot)

    @pl.loop(0, 2 * zs)
    def _(k):
        slot, copy = hc_copy(k % zs, 1 - c, (k // zs + y) % 2)
        copy.wait_recv()
        take(slot)

    out_ref[...] = out_t[...].T

    @pl.loop(0, 2 * zs)
    def _(j):
        core_copy(j).wait_send()

    @pl.loop(0, zs)
    def _(k):
        y_copy(k).wait_send()

    @pl.loop(1, zs)
    def _(i):
        z_copy(i).wait_send()
        hz_copy(i).wait_send()

    @pl.loop(0, zs)
    def _(i):
        hy_copy(i, y)[1].wait_send()
        hc_copy(i, c, y)[1].wait_send()
        hc_copy(i, c, 1 - y)[1].wait_send()


def solution(mesh):
    n = mesh.shape["col"]
    zs = n // 4

    def body(features, block_values, block_owner, block_sub, block_col, block_valid, norm_gain,
             weight):
        nb, bs = block_values.shape[:2]
        rows, width = features.shape
        smem = pl.BlockSpec(memory_space=pltpu.SMEM)
        vmem = pl.BlockSpec(memory_space=pltpu.VMEM)
        blocks = jax.ShapeDtypeStruct((n, rows, rows), jnp.bfloat16)
        hi, lo = pl.pallas_call(
            functools.partial(merge_kernel, n, bs, nb),
            out_shape=(blocks, blocks),
            in_specs=[smem] * 4 + [pl.BlockSpec(memory_space=pl.ANY)],
            out_specs=(vmem, vmem),
            scratch_shapes=[
                pltpu.VMEM((n, rows, rows), jnp.float32),
                pltpu.VMEM((nb, bs, bs), jnp.bfloat16),
                pltpu.SemaphoreType.DMA((CHUNKS,)),
            ],
            compiler_params=pltpu.CompilerParams(vmem_limit_bytes=44 * MIB),
        )(block_owner[:, 0], block_sub, block_col, block_valid, block_values)

        f32, bf16 = jnp.float32, jnp.bfloat16
        dma = pltpu.SemaphoreType.DMA
        return pl.pallas_call(
            functools.partial(layer_kernel, n),
            out_shape=jax.ShapeDtypeStruct((rows, width), f32),
            in_specs=[vmem] * 5,
            out_specs=vmem,
            scratch_shapes=[
                pltpu.VMEM((2 * zs, rows, width), f32),
                pltpu.VMEM((2 * zs, rows, width), f32),
                pltpu.VMEM((zs, rows, width), bf16),
                pltpu.VMEM((zs, rows, width), bf16),
                pltpu.VMEM((zs, rows, width), bf16),
                pltpu.VMEM((zs, rows, width), bf16),
                pltpu.VMEM((2 * zs, rows, width), f32),
                pltpu.VMEM((rows, width), f32),
                pltpu.VMEM((n, width, rows), bf16),
                pltpu.VMEM((width, rows), f32),
                dma((2 * zs,)), dma((2 * zs,)), dma((zs,)), dma((zs,)), dma((zs,)), dma((zs,)),
                dma((zs,)), dma((zs,)), dma((zs,)), dma((zs,)), dma((2 * zs,)), dma((2 * zs,)),
            ],
            compiler_params=pltpu.CompilerParams(
                collective_id=0, has_side_effects=True, vmem_limit_bytes=60 * MIB),
        )(hi, lo, features, norm_gain[None, :], weight)

    placed = (
        P(("groups", "col"), None),
        P(("groups", "col"), None, None),
        P(("groups", "col"), None),
        P(("groups", "col")),
        P(("groups", "col")),
        P(("groups", "col")),
        P(),
        P(),
    )
    return jax.shard_map(
        body, mesh=mesh, in_specs=placed, out_specs=P(("groups", "col"), None), check_vma=False
    )
```

```python
import functools

import jax
import jax.numpy as jnp
from jax import lax
from jax.experimental import pallas as pl
from jax.experimental.pallas import tpu as pltpu
from jax.sharding import PartitionSpec as P

MIB = 1024 * 1024
CHUNKS = 8


def merge_kernel(n, bs, nb, owner_hbm, sub_hbm, col_hbm, valid_hbm, values_ref, hi_ref, lo_ref,
                 dense, staged, owner_ref, sub_ref, col_ref, valid_ref, sems, index_sems):
    zs = n // 4
    per = nb // CHUNKS

    def chunk(i):
        part = pl.ds(i * per, per)
        return pltpu.make_async_copy(values_ref.at[part], staged.at[part], sems.at[i])

    indices = [
        pltpu.make_async_copy(src, dst, index_sems.at[i])
        for i, (src, dst) in enumerate((
            (owner_hbm, owner_ref), (sub_hbm, sub_ref), (col_hbm, col_ref), (valid_hbm, valid_ref)))
    ]
    for copy in indices:
        copy.start()
    for i in range(CHUNKS):
        chunk(i).start()

    @pl.loop(0, n)
    def _(d):
        dense[d] = jnp.zeros(dense.shape[1:], jnp.float32)

    for copy in indices:
        copy.wait()

    for i in range(CHUNKS):
        chunk(i).wait()

        @pl.loop(i * per, (i + 1) * per)
        def _(s):
            owner = owner_ref[s]
            place = (owner % 2 * 2 + owner // 2 % 2) * zs + owner // 4
            rows = pl.ds(pl.multiple_of(sub_ref[s] * bs, bs), bs)
            columns = pl.ds(pl.multiple_of(col_ref[s] * bs, bs), bs)
            live = valid_ref[s].astype(jnp.float32)
            dense[place, rows, columns] += staged[s].astype(jnp.float32) * live

    @pl.loop(0, n)
    def _(d):
        whole = dense[d]
        head = whole.astype(jnp.bfloat16)
        hi_ref[d] = head
        lo_ref[d] = (whole - head.astype(jnp.float32)).astype(jnp.bfloat16)


def layer_kernel(n, cut, hi_ref, lo_ref, x_ref, gain_ref, w_ref, out_ref,
                 pa_send, pa_recv, yb_send, yb_recv, zb_send, zb_recv, acc, agg, hbuf, out_t,
                 pa_ss, pa_rs, yb_ss, yb_rs, zb_ss, zb_rs, hz_ss, hz_rs, hy_ss, hy_rs, hc_ss, hc_rs):
    zs = n // 4
    me = lax.axis_index("col")
    z, y, c = me // 4, me // 2 % 2, me % 2
    other_core = me + 1 - 2 * c
    other_y = me + 2 - 4 * y

    def dest(z_to):
        return z_to * 4 + y * 2 + c

    barrier = pltpu.get_barrier_semaphore()

    def greet(device):
        pl.semaphore_signal(barrier, inc=1, device_id={"col": device},
                            device_id_type=pl.DeviceIdType.MESH)

    greet(other_core)
    greet(other_y)
    for i in range(1, zs):
        greet(dest((z + i) % zs))
    pl.semaphore_wait(barrier, zs + 1)

    def remote(src, dst, ss, rs, device):
        return pltpu.make_async_remote_copy(
            src_ref=src, dst_ref=dst, send_sem=ss, recv_sem=rs,
            device_id={"col": device}, device_id_type=pl.DeviceIdType.MESH)

    def product(place):
        x = x_ref[...]
        return (jnp.dot(hi_ref[place], x, preferred_element_type=jnp.float32)
                + jnp.dot(lo_ref[place], x, preferred_element_type=jnp.float32))

    def core_copy(j):
        return remote(pa_send.at[j], pa_recv.at[j], pa_ss.at[j], pa_rs.at[j], other_core)

    def turned(k):
        return (k + (1 - y) * zs) % (2 * zs)

    @pl.loop(0, 2 * zs)
    def _(k):
        j = turned(k)
        pa_send[j] = product((1 - c) * 2 * zs + j)
        core_copy(j).start()

    @pl.loop(0, 2 * zs)
    def _(k):
        j = turned(k)
        acc[j] = product(c * 2 * zs + j)

    def y_copy(k):
        return remote(yb_send.at[k], yb_recv.at[k], yb_ss.at[k], yb_rs.at[k], other_y)

    @pl.loop(0, zs)
    def _(k):
        k = (z + 1 + k) % zs
        j = (1 - y) * zs + k
        core_copy(j).wait_recv()
        yb_send[k] = (acc[j] + pa_recv[j]).astype(jnp.bfloat16)
        y_copy(k).start()

    @pl.loop(0, zs)
    def _(k):
        j = y * zs + k
        core_copy(j).wait_recv()
        acc[j] = acc[j] + pa_recv[j]

    def z_copy(i):
        return remote(zb_send.at[i], zb_recv.at[i], zb_ss.at[i], zb_rs.at[i], dest((z + i) % zs))

    @pl.loop(1, zs)
    def _(i):
        k = (z + i) % zs
        y_copy(k).wait_recv()
        zb_send[i] = (acc[y * zs + k] + yb_recv[k].astype(jnp.float32)).astype(jnp.bfloat16)
        z_copy(i).start()

    y_copy(z).wait_recv()
    agg[...] = acc[y * zs + z] + yb_recv[z].astype(jnp.float32)

    @pl.loop(1, zs)
    def _(i):
        z_copy(i).wait_recv()
        agg[...] += zb_recv[i].astype(jnp.float32)

    total = agg[...]
    scale = lax.rsqrt(jnp.mean(total * total, axis=1, keepdims=True) + 1e-06)
    normed = (total * scale * gain_ref[...]).astype(jnp.bfloat16)
    hidden = jnp.maximum(jnp.dot(normed, w_ref[...], preferred_element_type=jnp.float32), 0.0)
    mine = (c * 2 + y) * zs + z
    hbuf[mine] = hidden.T.astype(jnp.bfloat16)

    parts = (pl.ds(0, cut), pl.ds(cut, hbuf.shape[1] - cut))

    def slot_of(c_of, y_of, z_of):
        return (c_of * 2 + y_of) * zs + z_of

    STREAMS = ((0, y), (1, y), (1, 1 - y))

    def chain(stream, z_of, way):
        part, y_of = STREAMS[stream]
        ref = hbuf.at[slot_of(c, y_of, z_of), parts[part]]
        return remote(ref, ref, hz_ss.at[way * 3 * zs + stream * zs + z_of],
                      hz_rs.at[stream * zs + z_of], dest((z + 1 - 2 * way + zs) % zs))

    def across(part, y_of, z_of):
        ref = hbuf.at[slot_of(c, y_of, z_of), parts[part]]
        k = z_of if part == 0 else zs
        return remote(ref, ref, hy_ss.at[k], hy_rs.at[k], other_y)

    def pair(part, c_of, y_of, z_of):
        slot = slot_of(c_of, y_of, z_of)
        ref = hbuf.at[slot, parts[part]]
        k = part * 2 * zs + y_of * zs + z_of
        return remote(ref, ref, hc_ss.at[k], hc_rs.at[k], other_core)

    out_t[...] = jnp.zeros(out_t.shape, jnp.float32)

    def take(slot):
        out_t[...] += (jnp.dot(hbuf[slot], hi_ref[slot], preferred_element_type=jnp.float32)
                       + jnp.dot(hbuf[slot], lo_ref[slot], preferred_element_type=jnp.float32))

    def can_go(way):
        return z + 1 < zs if way == 0 else z > 0

    def take_other(z_of):
        for y_of in (y, 1 - y):
            for part in (0, 1):
                pair(part, 1 - c, y_of, z_of).wait_recv()
            take(slot_of(1 - c, y_of, z_of))

    across(1, y, z).start()
    for way in (0, 1):
        @pl.when(can_go(way))
        def _():
            chain(0, z, way).start()
            chain(1, z, way).start()
    across(0, y, z).start()
    pair(0, c, y, z).start()
    pair(1, c, y, z).start()
    across(1, 1 - y, z).wait_recv()
    for way in (0, 1):
        @pl.when(can_go(way))
        def _():
            chain(2, z, way).start()
    pair(1, c, 1 - y, z).start()
    take(mine)
    across(0, 1 - y, z).wait_recv()
    pair(0, c, 1 - y, z).start()
    take(slot_of(c, 1 - y, z))

    def has(way, i):
        return z - i >= 0 if way == 0 else z + i < zs

    def came(way, i):
        return z - i if way == 0 else z + i

    def both_ways(i, do):
        for way in (0, 1):
            @pl.when(has(way, i))
            def _():
                do(way, came(way, i))

    @pl.loop(1, zs)
    def _(i):
        for stream in (0, 1, 2):
            def arrive(way, z_of):
                chain(stream, z_of, way).wait_recv()

                @pl.when(can_go(way))
                def _():
                    chain(stream, z_of, way).start()

                part, y_of = STREAMS[stream]
                if stream == 0:
                    across(0, y, z_of).start()
                pair(part, c, y_of, z_of).start()

            both_ways(i, arrive)

        both_ways(i, lambda way, z_of: take(slot_of(c, y, z_of)))

        def far(way, z_of):
            across(0, 1 - y, z_of).wait_recv()
            pair(0, c, 1 - y, z_of).start()
            take(slot_of(c, 1 - y, z_of))

        both_ways(i, far)

        @pl.when(i == 1)
        def _():
            take_other(z)

        @pl.when(i > 1)
        def _():
            both_ways(i - 1, lambda way, z_of: take_other(z_of))

    both_ways(zs - 1, lambda way, z_of: take_other(z_of))

    out_ref[...] = out_t[...]

    @pl.loop(0, 2 * zs)
    def _(j):
        core_copy(j).wait_send()

    @pl.loop(0, zs)
    def _(k):
        y_copy(k).wait_send()

    @pl.loop(1, zs)
    def _(i):
        z_copy(i).wait_send()

    across(1, y, z).wait_send()

    @pl.loop(0, zs)
    def _(k):
        across(0, y, k).wait_send()
        for y_of in (0, 1):
            for part in (0, 1):
                pair(part, c, y_of, k).wait_send()
        for way in (0, 1):
            from_there = k <= z if way == 0 else k >= z

            @pl.when(can_go(way) & from_there)
            def _():
                for stream in (0, 1, 2):
                    chain(stream, k, way).wait_send()


def solution(mesh):
    n = mesh.shape["col"]
    zs = n // 4

    def body(features, block_values, block_owner, block_sub, block_col, block_valid, norm_gain,
             weight):
        nb, bs = block_values.shape[:2]
        rows, width = features.shape
        hbm = pl.BlockSpec(memory_space=pltpu.HBM)
        vmem_limit = (n + 6) * 7 // 8 * MIB
        vmem = pl.BlockSpec(memory_space=pltpu.VMEM)
        blocks = jax.ShapeDtypeStruct((n, rows, rows), jnp.bfloat16)
        hi, lo = pl.pallas_call(
            functools.partial(merge_kernel, n, bs, nb),
            out_shape=(blocks, blocks),
            in_specs=[hbm] * 5,
            out_specs=(vmem, vmem),
            scratch_shapes=[
                pltpu.VMEM((n, rows, rows), jnp.float32),
                pltpu.VMEM((nb, bs, bs), jnp.bfloat16),
            ] + [pltpu.SMEM((nb,), jnp.int32)] * 4 + [
                pltpu.SemaphoreType.DMA((CHUNKS,)),
                pltpu.SemaphoreType.DMA((4,)),
            ],
            compiler_params=pltpu.CompilerParams(vmem_limit_bytes=vmem_limit),
        )(block_owner[:, 0], block_sub, block_col, block_valid, block_values)

        f32, bf16 = jnp.float32, jnp.bfloat16
        dma = pltpu.SemaphoreType.DMA
        return pl.pallas_call(
            functools.partial(layer_kernel, n, width * 5 // 8),
            out_shape=jax.ShapeDtypeStruct((width, rows), f32),
            in_specs=[vmem] * 5,
            out_specs=vmem,
            scratch_shapes=[
                pltpu.VMEM((2 * zs, rows, width), f32),
                pltpu.VMEM((2 * zs, rows, width), f32),
                pltpu.VMEM((zs, rows, width), bf16),
                pltpu.VMEM((zs, rows, width), bf16),
                pltpu.VMEM((zs, rows, width), bf16),
                pltpu.VMEM((zs, rows, width), bf16),
                pltpu.VMEM((2 * zs, rows, width), f32),
                pltpu.VMEM((rows, width), f32),
                pltpu.VMEM((n, width, rows), bf16),
                pltpu.VMEM((width, rows), f32),
                dma((2 * zs,)), dma((2 * zs,)), dma((zs,)), dma((zs,)), dma((zs,)), dma((zs,)),
                dma((6 * zs,)), dma((3 * zs,)), dma((zs + 1,)), dma((zs + 1,)),
                dma((4 * zs,)), dma((4 * zs,)),
            ],
            compiler_params=pltpu.CompilerParams(
                collective_id=0, has_side_effects=True, vmem_limit_bytes=vmem_limit),
        )(hi, lo, features, norm_gain[None, :], weight).T

    placed = (
        P(("groups", "col"), None),
        P(("groups", "col"), None, None),
        P(("groups", "col"), None),
        P(("groups", "col")),
        P(("groups", "col")),
        P(("groups", "col")),
        P(),
        P(),
    )
    return jax.shard_map(
        body, mesh=mesh, in_specs=placed, out_specs=P(("groups", "col"), None), check_vma=False
    )
```

```python
import functools

import jax
import jax.numpy as jnp
from jax import lax
from jax.experimental import pallas as pl
from jax.experimental.pallas import tpu as pltpu
from jax.sharding import PartitionSpec as P

MIB = 1024 * 1024
CHUNKS = 8
CUTS = (7, 6, 3)


def merge_kernel(bs, nb, index_any, values_ref, hi_ref, lo_ref, dense, staged, index_ref, sems,
                 index_sem):
    n = dense.shape[0]
    per = nb // CHUNKS

    def chunk(i):
        part = pl.ds(i * per, per)
        return pltpu.make_async_copy(values_ref.at[part], staged.at[part], sems.at[i])

    index_copy = pltpu.make_async_copy(index_any, index_ref, index_sem)
    index_copy.start()
    for i in range(CHUNKS):
        chunk(i).start()

    @pl.loop(0, n)
    def _(d):
        dense[d] = jnp.zeros(dense.shape[1:], jnp.float32)

    index_copy.wait()

    for i in range(CHUNKS):
        chunk(i).wait()

        @pl.loop(i * per, (i + 1) * per)
        def _(s):
            index = index_ref[s]
            place = index // 8
            rows = pl.ds(pl.multiple_of(index // 4 % 2 * bs, bs), bs)
            columns = pl.ds(pl.multiple_of(index // 2 % 2 * bs, bs), bs)
            live = (index % 2).astype(jnp.float32)
            dense[place, rows, columns] += staged[s].astype(jnp.float32) * live

    @pl.loop(0, n)
    def _(d):
        whole = dense[d]
        head = whole.astype(jnp.bfloat16)
        hi_ref[d] = head
        lo_ref[d] = (whole - head.astype(jnp.float32)).astype(jnp.bfloat16)


def layer_kernel(n, cuts, hi_ref, lo_ref, x_ref, gain_ref, w_ref, out_ref,
                 pa_send, pa_recv, yb_send, yb_recv, zb_send, zb_recv, acc, agg, hbuf, out_t,
                 pa_ss, pa_rs, yb_ss, yb_rs, zb_ss, zb_rs, hz_ss, hz_rs, hy_ss, hy_rs, hc_ss, hc_rs):
    zs = n // 4
    me = lax.axis_index("col")
    z, y, c = me // 4, me // 2 % 2, me % 2
    other_core = me + 1 - 2 * c
    other_y = me + 2 - 4 * y

    def dest(z_to):
        return z_to * 4 + y * 2 + c

    barrier = pltpu.get_barrier_semaphore()

    def greet(device):
        pl.semaphore_signal(barrier, inc=1, device_id={"col": device},
                            device_id_type=pl.DeviceIdType.MESH)

    greet(other_core)
    greet(other_y)
    for i in range(1, zs):
        greet(dest((z + i) % zs))

    def remote(src, dst, ss, rs, device):
        return pltpu.make_async_remote_copy(
            src_ref=src, dst_ref=dst, send_sem=ss, recv_sem=rs,
            device_id={"col": device}, device_id_type=pl.DeviceIdType.MESH)

    def product(place):
        x = x_ref[...]
        return (jnp.dot(hi_ref[place], x, preferred_element_type=jnp.float32)
                + jnp.dot(lo_ref[place], x, preferred_element_type=jnp.float32))

    def core_copy(j):
        return remote(pa_send.at[j], pa_recv.at[j], pa_ss.at[j], pa_rs.at[j], other_core)

    def turned(k):
        return (k + (1 - y) * zs) % (2 * zs)

    @pl.loop(0, 2 * zs)
    def _(k):
        j = turned(k)
        pa_send[j] = product((1 - c) * 2 * zs + j)

    pl.semaphore_wait(barrier, zs + 1)

    @pl.loop(0, 2 * zs)
    def _(k):
        core_copy(turned(k)).start()

    @pl.loop(0, 2 * zs)
    def _(k):
        j = turned(k)
        acc[j] = product(c * 2 * zs + j)

    def y_copy(k):
        return remote(yb_send.at[k], yb_recv.at[k], yb_ss.at[k], yb_rs.at[k], other_y)

    @pl.loop(0, zs)
    def _(k):
        k = (z + 1 + k) % zs
        j = (1 - y) * zs + k
        core_copy(j).wait_recv()
        yb_send[k] = (acc[j] + pa_recv[j]).astype(jnp.bfloat16)
        y_copy(k).start()

    @pl.loop(0, zs)
    def _(k):
        j = y * zs + k
        core_copy(j).wait_recv()
        acc[j] = acc[j] + pa_recv[j]

    def z_copy(i):
        return remote(zb_send.at[i], zb_recv.at[i], zb_ss.at[i], zb_rs.at[i], dest((z + i) % zs))

    @pl.loop(1, zs)
    def _(i):
        k = (z + i) % zs
        y_copy(k).wait_recv()
        zb_send[i] = (acc[y * zs + k] + yb_recv[k].astype(jnp.float32)).astype(jnp.bfloat16)
        z_copy(i).start()

    y_copy(z).wait_recv()
    agg[...] = acc[y * zs + z] + yb_recv[z].astype(jnp.float32)

    @pl.loop(1, zs)
    def _(i):
        z_copy(i).wait_recv()
        agg[...] += zb_recv[i].astype(jnp.float32)

    total = agg[...]
    scale = lax.rsqrt(jnp.mean(total * total, axis=1, keepdims=True) + 1e-06)
    normed = (total * scale * gain_ref[...]).astype(jnp.bfloat16)
    hidden = jnp.maximum(jnp.dot(normed, w_ref[...], preferred_element_type=jnp.float32), 0.0)
    mine = (c * 2 + y) * zs + z
    hbuf[mine] = hidden.T.astype(jnp.bfloat16)

    last = len(cuts) - 1
    pieces = [pl.ds(sum(cuts[:i]), cuts[i]) for i in range(len(cuts))]
    streams = [(p, y) for p in range(len(cuts))] + [(last, 1 - y)]

    def slot_of(c_of, y_of, z_of):
        return (c_of * 2 + y_of) * zs + z_of

    def chain(stream, z_of, way):
        piece, y_of = streams[stream]
        ref = hbuf.at[slot_of(c, y_of, z_of), pieces[piece]]
        return remote(ref, ref, hz_ss.at[(way * len(streams) + stream) * zs + z_of],
                      hz_rs.at[stream * zs + z_of], dest((z + 1 - 2 * way + zs) % zs))

    def across(piece, y_of, z_of):
        ref = hbuf.at[slot_of(c, y_of, z_of), pieces[piece]]
        k = piece * zs + z_of if piece < last else last * zs
        return remote(ref, ref, hy_ss.at[k], hy_rs.at[k], other_y)

    def pair(piece, c_of, y_of, z_of):
        ref = hbuf.at[slot_of(c_of, y_of, z_of), pieces[piece]]
        k = (piece * 2 + y_of) * zs + z_of
        return remote(ref, ref, hc_ss.at[k], hc_rs.at[k], other_core)

    def take(slot):
        out_t[...] += (jnp.dot(hbuf[slot], hi_ref[slot], preferred_element_type=jnp.float32)
                       + jnp.dot(hbuf[slot], lo_ref[slot], preferred_element_type=jnp.float32))

    def can_go(way):
        return z + 1 < zs if way == 0 else z > 0

    def both_ways(i, first, end, do):
        for way in (0, 1):
            z_of = z - i if way == 0 else z + i
            there = (z_of >= 0) if way == 0 else (z_of < zs) & (i > 0)

            @pl.when(there & (i >= first) & (i < end))
            def _():
                do(way, z_of)

    def go_on(stream, z_of, way):
        @pl.when(can_go(way))
        def _():
            chain(stream, z_of, way).start()

    across(last, y, z).start()
    for p in range(len(cuts)):
        for way in (0, 1):
            go_on(p, z, way)
        if p < last:
            across(p, y, z).start()
    for p in range(len(cuts)):
        pair(p, c, y, z).start()
    out_t[...] = jnp.zeros(out_t.shape, jnp.float32)
    take(mine)
    across(last, 1 - y, z).wait_recv()
    for way in (0, 1):
        go_on(len(cuts), z, way)
    pair(last, c, 1 - y, z).start()

    @pl.loop(1, zs + 2)
    def _(i):
        for stream in range(len(streams)):
            def arrive(way, z_of):
                chain(stream, z_of, way).wait_recv()
                go_on(stream, z_of, way)
                piece, y_of = streams[stream]
                if piece < last:
                    across(piece, y, z_of).start()
                pair(piece, c, y_of, z_of).start()

            both_ways(i, 1, zs, arrive)

        both_ways(i, 1, zs, lambda way, z_of: take(slot_of(c, y, z_of)))

        def far(way, z_of):
            for p in range(last):
                across(p, 1 - y, z_of).wait_recv()
                pair(p, c, 1 - y, z_of).start()
            take(slot_of(c, 1 - y, z_of))

        both_ways(i - 1, 0, zs, far)

        def other(way, z_of):
            for y_of in (y, 1 - y):
                for p in range(len(cuts)):
                    pair(p, 1 - c, y_of, z_of).wait_recv()
                take(slot_of(1 - c, y_of, z_of))

        both_ways(i - 2, 0, zs, other)

    out_ref[...] = out_t[...]

    @pl.loop(0, 2 * zs)
    def _(j):
        core_copy(j).wait_send()

    @pl.loop(0, zs)
    def _(k):
        y_copy(k).wait_send()

    @pl.loop(1, zs)
    def _(i):
        z_copy(i).wait_send()

    across(last, y, z).wait_send()

    @pl.loop(0, zs)
    def _(k):
        for p in range(len(cuts)):
            if p < last:
                across(p, y, k).wait_send()
            for y_of in (0, 1):
                pair(p, c, y_of, k).wait_send()
        for way in (0, 1):
            from_there = k <= z if way == 0 else k >= z

            @pl.when(can_go(way) & from_there)
            def _():
                for stream in range(len(streams)):
                    chain(stream, k, way).wait_send()


def solution(mesh):
    n = mesh.shape["col"]
    zs = n // 4

    def body(features, block_values, block_owner, block_sub, block_col, block_valid, norm_gain,
             weight):
        nb, bs = block_values.shape[:2]
        rows, width = features.shape
        anywhere = pl.BlockSpec(memory_space=pl.ANY)
        vmem_limit = (n + 6) * 7 // 8 * MIB
        vmem = pl.BlockSpec(memory_space=pltpu.VMEM)
        owner = block_owner[:, 0]
        place = (owner % 2 * 2 + owner // 2 % 2) * zs + owner // 4
        index = ((place * 2 + block_sub) * 2 + block_col) * 2 + block_valid
        blocks = jax.ShapeDtypeStruct((n, rows, rows), jnp.bfloat16)
        hi, lo = pl.pallas_call(
            functools.partial(merge_kernel, bs, nb),
            out_shape=(blocks, blocks),
            in_specs=[anywhere] * 2,
            out_specs=(vmem, vmem),
            scratch_shapes=[
                pltpu.VMEM((n, rows, rows), jnp.float32),
                pltpu.VMEM((nb, bs, bs), jnp.bfloat16),
                pltpu.SMEM((nb,), jnp.int32),
                pltpu.SemaphoreType.DMA((CHUNKS,)),
                pltpu.SemaphoreType.DMA,
            ],
            compiler_params=pltpu.CompilerParams(vmem_limit_bytes=vmem_limit),
        )(index, block_values)

        f32, bf16 = jnp.float32, jnp.bfloat16
        cuts = tuple(width // 16 * part for part in CUTS)
        count = len(cuts)
        dma = pltpu.SemaphoreType.DMA
        return pl.pallas_call(
            functools.partial(layer_kernel, n, cuts),
            out_shape=jax.ShapeDtypeStruct((width, rows), f32),
            in_specs=[vmem] * 5,
            out_specs=vmem,
            scratch_shapes=[
                pltpu.VMEM((2 * zs, rows, width), f32),
                pltpu.VMEM((2 * zs, rows, width), f32),
                pltpu.VMEM((zs, rows, width), bf16),
                pltpu.VMEM((zs, rows, width), bf16),
                pltpu.VMEM((zs, rows, width), bf16),
                pltpu.VMEM((zs, rows, width), bf16),
                pltpu.VMEM((2 * zs, rows, width), f32),
                pltpu.VMEM((rows, width), f32),
                pltpu.VMEM((n, width, rows), bf16),
                pltpu.VMEM((width, rows), f32),
                dma((2 * zs,)), dma((2 * zs,)), dma((zs,)), dma((zs,)), dma((zs,)), dma((zs,)),
                dma((2 * (count + 1) * zs,)), dma(((count + 1) * zs,)),
                dma(((count - 1) * zs + 1,)), dma(((count - 1) * zs + 1,)),
                dma((2 * count * zs,)), dma((2 * count * zs,)),
            ],
            compiler_params=pltpu.CompilerParams(
                collective_id=0, has_side_effects=True, vmem_limit_bytes=vmem_limit),
        )(hi, lo, features, norm_gain[None, :], weight).T

    placed = (
        P(("groups", "col"), None),
        P(("groups", "col"), None, None),
        P(("groups", "col"), None),
        P(("groups", "col")),
        P(("groups", "col")),
        P(("groups", "col")),
        P(),
        P(),
    )
    return jax.shard_map(
        body, mesh=mesh, in_specs=placed, out_specs=P(("groups", "col"), None), check_vma=False
    )
```

```python
import functools

import jax
import jax.numpy as jnp
from jax import lax
from jax.experimental import pallas as pl
from jax.experimental.pallas import tpu as pltpu
from jax.sharding import PartitionSpec as P

MIB = 1024 * 1024
CHUNKS = 8
CUTS = (7, 6, 3)


def merge_kernel(bs, nb, index_any, values_ref, hi_ref, lo_ref, dense, staged, index_ref, sems,
                 index_sem):
    n = dense.shape[0]
    per = nb // CHUNKS

    def chunk(i):
        part = pl.ds(i * per, per)
        return pltpu.make_async_copy(values_ref.at[part], staged.at[part], sems.at[i])

    index_copy = pltpu.make_async_copy(index_any, index_ref, index_sem)
    index_copy.start()
    for i in range(CHUNKS):
        chunk(i).start()

    @pl.loop(0, n)
    def _(d):
        dense[d] = jnp.zeros(dense.shape[1:], jnp.float32)

    index_copy.wait()

    for i in range(CHUNKS):
        chunk(i).wait()

        @pl.loop(i * per, (i + 1) * per)
        def _(s):
            index = index_ref[s]
            place = index // 8
            rows = pl.ds(pl.multiple_of(index // 4 % 2 * bs, bs), bs)
            columns = pl.ds(pl.multiple_of(index // 2 % 2 * bs, bs), bs)
            live = (index % 2).astype(jnp.float32)
            dense[place, rows, columns] += staged[s].astype(jnp.float32) * live

    @pl.loop(0, n)
    def _(d):
        whole = dense[d]
        head = whole.astype(jnp.bfloat16)
        hi_ref[d] = head
        lo_ref[d] = (whole - head.astype(jnp.float32)).astype(jnp.bfloat16)


def layer_kernel(n, cuts, hi_ref, lo_ref, x_ref, gain_ref, w_ref, out_ref,
                 pa_send, pa_recv, yb_send, yb_recv, zb_send, zb_recv, acc, agg, hbuf, out_t,
                 pa_ss, pa_rs, yb_ss, yb_rs, zb_ss, zb_rs, hz_ss, hz_rs, hy_ss, hy_rs, hc_ss, hc_rs):
    zs = n // 4
    me = lax.axis_index("col")
    z, y, c = me // 4, me // 2 % 2, me % 2
    other_core = me + 1 - 2 * c
    other_y = me + 2 - 4 * y

    def dest(z_to):
        return z_to * 4 + y * 2 + c

    barrier = pltpu.get_barrier_semaphore()

    def greet(device):
        pl.semaphore_signal(barrier, inc=1, device_id={"col": device},
                            device_id_type=pl.DeviceIdType.MESH)

    greet(other_core)
    greet(other_y)
    for i in range(1, zs):
        greet(dest((z + i) % zs))

    def remote(src, dst, ss, rs, device):
        return pltpu.make_async_remote_copy(
            src_ref=src, dst_ref=dst, send_sem=ss, recv_sem=rs,
            device_id={"col": device}, device_id_type=pl.DeviceIdType.MESH)

    def product(place):
        x = x_ref[...]
        return (jnp.dot(hi_ref[place], x, preferred_element_type=jnp.float32)
                + jnp.dot(lo_ref[place], x, preferred_element_type=jnp.float32))

    def core_copy(j):
        return remote(pa_send.at[j], pa_recv.at[j], pa_ss.at[j], pa_rs.at[j], other_core)

    @pl.loop(0, zs)
    def _(k):
        j = (1 - y) * zs + (z + 1 + k) % zs
        pa_send[j] = product((1 - c) * 2 * zs + j)

    pl.semaphore_wait(barrier, zs + 1)

    @pl.loop(0, zs)
    def _(k):
        core_copy((1 - y) * zs + (z + 1 + k) % zs).start()

    half = acc.shape[1] // 2
    halves = (pl.ds(0, half), pl.ds(half, half))

    def y_copy(k, h):
        return remote(yb_send.at[k, halves[h]], yb_recv.at[k, halves[h]],
                      yb_ss.at[2 * k + h], yb_rs.at[2 * k + h], other_y)

    @pl.loop(0, zs)
    def _(k):
        k = (z + 1 + k) % zs
        j = (1 - y) * zs + k
        acc[j] = product(c * 2 * zs + j)
        core_copy(j).wait_recv()
        for h in (0, 1):
            yb_send[k, halves[h]] = (acc[j, halves[h]] + pa_recv[j, halves[h]]).astype(jnp.bfloat16)
            y_copy(k, h).start()

    @pl.loop(0, zs)
    def _(k):
        j = y * zs + (z + 1 + k) % zs
        pa_send[j] = product((1 - c) * 2 * zs + j)
        core_copy(j).start()

    @pl.loop(0, zs)
    def _(k):
        j = y * zs + (z + 1 + k) % zs
        acc[j] = product(c * 2 * zs + j)
        core_copy(j).wait_recv()
        acc[j] = acc[j] + pa_recv[j]

    def z_copy(i, h):
        return remote(zb_send.at[i, halves[h]], zb_recv.at[i, halves[h]],
                      zb_ss.at[2 * i + h], zb_rs.at[2 * i + h], dest((z + i) % zs))

    @pl.loop(1, zs)
    def _(i):
        k = (z + i) % zs
        for h in (0, 1):
            y_copy(k, h).wait_recv()
            zb_send[i, halves[h]] = (
                acc[y * zs + k, halves[h]] + yb_recv[k, halves[h]].astype(jnp.float32)
            ).astype(jnp.bfloat16)
            z_copy(i, h).start()

    for h in (0, 1):
        y_copy(z, h).wait_recv()
    agg[...] = acc[y * zs + z] + yb_recv[z].astype(jnp.float32)

    @pl.loop(1, zs)
    def _(i):
        for h in (0, 1):
            z_copy(i, h).wait_recv()
        agg[...] += zb_recv[i].astype(jnp.float32)

    total = agg[...]
    scale = lax.rsqrt(jnp.mean(total * total, axis=1, keepdims=True) + 1e-06)
    normed = (total * scale * gain_ref[...]).astype(jnp.bfloat16)
    hidden = jnp.maximum(jnp.dot(normed, w_ref[...], preferred_element_type=jnp.float32), 0.0)
    mine = (c * 2 + y) * zs + z
    hbuf[mine] = hidden.T.astype(jnp.bfloat16)

    last = len(cuts) - 1
    pieces = [pl.ds(sum(cuts[:i]), cuts[i]) for i in range(len(cuts))]
    streams = [(p, y) for p in range(len(cuts))] + [(last, 1 - y)]

    def slot_of(c_of, y_of, z_of):
        return (c_of * 2 + y_of) * zs + z_of

    def chain(stream, z_of, way):
        piece, y_of = streams[stream]
        ref = hbuf.at[slot_of(c, y_of, z_of), pieces[piece]]
        return remote(ref, ref, hz_ss.at[(way * len(streams) + stream) * zs + z_of],
                      hz_rs.at[stream * zs + z_of], dest((z + 1 - 2 * way + zs) % zs))

    def across(piece, y_of, z_of):
        ref = hbuf.at[slot_of(c, y_of, z_of), pieces[piece]]
        k = piece * zs + z_of if piece < last else last * zs
        return remote(ref, ref, hy_ss.at[k], hy_rs.at[k], other_y)

    def pair(piece, c_of, y_of, z_of):
        ref = hbuf.at[slot_of(c_of, y_of, z_of), pieces[piece]]
        k = (piece * 2 + y_of) * zs + z_of
        return remote(ref, ref, hc_ss.at[k], hc_rs.at[k], other_core)

    def take(slot):
        out_t[...] += (jnp.dot(hbuf[slot], hi_ref[slot], preferred_element_type=jnp.float32)
                       + jnp.dot(hbuf[slot], lo_ref[slot], preferred_element_type=jnp.float32))

    def can_go(way):
        return z + 1 < zs if way == 0 else z > 0

    def both_ways(i, first, end, do):
        for way in (0, 1):
            z_of = z - i if way == 0 else z + i
            there = (z_of >= 0) if way == 0 else (z_of < zs) & (i > 0)

            @pl.when(there & (i >= first) & (i < end))
            def _():
                do(way, z_of)

    def go_on(stream, z_of, way):
        @pl.when(can_go(way))
        def _():
            chain(stream, z_of, way).start()

    across(last, y, z).start()
    for p in range(len(cuts)):
        for way in (0, 1):
            go_on(p, z, way)
        if p < last:
            across(p, y, z).start()
    for p in range(len(cuts)):
        pair(p, c, y, z).start()
    out_t[...] = jnp.zeros(out_t.shape, jnp.float32)
    take(mine)
    across(last, 1 - y, z).wait_recv()
    for way in (0, 1):
        go_on(len(cuts), z, way)
    pair(last, c, 1 - y, z).start()

    @pl.loop(1, zs + 2)
    def _(i):
        for stream in range(len(streams)):
            def arrive(way, z_of):
                chain(stream, z_of, way).wait_recv()
                go_on(stream, z_of, way)
                piece, y_of = streams[stream]
                if piece < last:
                    across(piece, y, z_of).start()
                pair(piece, c, y_of, z_of).start()

            both_ways(i, 1, zs, arrive)

        both_ways(i, 1, zs, lambda way, z_of: take(slot_of(c, y, z_of)))

        def far(way, z_of):
            for p in range(last):
                across(p, 1 - y, z_of).wait_recv()
                pair(p, c, 1 - y, z_of).start()
            take(slot_of(c, 1 - y, z_of))

        both_ways(i - 1, 0, zs, far)

        def other(way, z_of):
            for y_of in (y, 1 - y):
                for p in range(len(cuts)):
                    pair(p, 1 - c, y_of, z_of).wait_recv()
                take(slot_of(1 - c, y_of, z_of))

        both_ways(i - 2, 0, zs, other)

    out_ref[...] = out_t[...]

    @pl.loop(0, 2 * zs)
    def _(j):
        core_copy(j).wait_send()

    @pl.loop(0, zs)
    def _(k):
        for h in (0, 1):
            y_copy(k, h).wait_send()

    @pl.loop(1, zs)
    def _(i):
        for h in (0, 1):
            z_copy(i, h).wait_send()

    across(last, y, z).wait_send()

    @pl.loop(0, zs)
    def _(k):
        for p in range(len(cuts)):
            if p < last:
                across(p, y, k).wait_send()
            for y_of in (0, 1):
                pair(p, c, y_of, k).wait_send()
        for way in (0, 1):
            from_there = k <= z if way == 0 else k >= z

            @pl.when(can_go(way) & from_there)
            def _():
                for stream in range(len(streams)):
                    chain(stream, k, way).wait_send()


def solution(mesh):
    n = mesh.shape["col"]
    zs = n // 4

    def body(features, block_values, block_owner, block_sub, block_col, block_valid, norm_gain,
             weight):
        nb, bs = block_values.shape[:2]
        rows, width = features.shape
        anywhere = pl.BlockSpec(memory_space=pl.ANY)
        vmem_limit = (n + 6) * 7 // 8 * MIB
        vmem = pl.BlockSpec(memory_space=pltpu.VMEM)
        owner = block_owner[:, 0]
        place = (owner % 2 * 2 + owner // 2 % 2) * zs + owner // 4
        index = ((place * 2 + block_sub) * 2 + block_col) * 2 + block_valid
        blocks = jax.ShapeDtypeStruct((n, rows, rows), jnp.bfloat16)
        hi, lo = pl.pallas_call(
            functools.partial(merge_kernel, bs, nb),
            out_shape=(blocks, blocks),
            in_specs=[anywhere] * 2,
            out_specs=(vmem, vmem),
            scratch_shapes=[
                pltpu.VMEM((n, rows, rows), jnp.float32),
                pltpu.VMEM((nb, bs, bs), jnp.bfloat16),
                pltpu.SMEM((nb,), jnp.int32),
                pltpu.SemaphoreType.DMA((CHUNKS,)),
                pltpu.SemaphoreType.DMA,
            ],
            compiler_params=pltpu.CompilerParams(vmem_limit_bytes=vmem_limit),
        )(index, block_values)

        f32, bf16 = jnp.float32, jnp.bfloat16
        cuts = tuple(width // 16 * part for part in CUTS)
        count = len(cuts)
        dma = pltpu.SemaphoreType.DMA
        return pl.pallas_call(
            functools.partial(layer_kernel, n, cuts),
            out_shape=jax.ShapeDtypeStruct((width, rows), f32),
            in_specs=[vmem] * 5,
            out_specs=vmem,
            scratch_shapes=[
                pltpu.VMEM((2 * zs, rows, width), f32),
                pltpu.VMEM((2 * zs, rows, width), f32),
                pltpu.VMEM((zs, rows, width), bf16),
                pltpu.VMEM((zs, rows, width), bf16),
                pltpu.VMEM((zs, rows, width), bf16),
                pltpu.VMEM((zs, rows, width), bf16),
                pltpu.VMEM((2 * zs, rows, width), f32),
                pltpu.VMEM((rows, width), f32),
                pltpu.VMEM((n, width, rows), bf16),
                pltpu.VMEM((width, rows), f32),
                dma((2 * zs,)), dma((2 * zs,)), dma((2 * zs,)), dma((2 * zs,)), dma((2 * zs,)),
                dma((2 * zs,)),
                dma((2 * (count + 1) * zs,)), dma(((count + 1) * zs,)),
                dma(((count - 1) * zs + 1,)), dma(((count - 1) * zs + 1,)),
                dma((2 * count * zs,)), dma((2 * count * zs,)),
            ],
            compiler_params=pltpu.CompilerParams(
                collective_id=0, has_side_effects=True, vmem_limit_bytes=vmem_limit),
        )(hi, lo, features, norm_gain[None, :], weight).T

    placed = (
        P(("groups", "col"), None),
        P(("groups", "col"), None, None),
        P(("groups", "col"), None),
        P(("groups", "col")),
        P(("groups", "col")),
        P(("groups", "col")),
        P(),
        P(),
    )
    return jax.shard_map(
        body, mesh=mesh, in_specs=placed, out_specs=P(("groups", "col"), None), check_vma=False
    )
```

```python
import functools

import jax
import jax.numpy as jnp
from jax import lax
from jax.experimental import pallas as pl
from jax.experimental.pallas import tpu as pltpu
from jax.sharding import PartitionSpec as P

MIB = 1024 * 1024
CHUNKS = 8
CUTS = (7, 6, 3)


def merge_kernel(bs, nb, index_any, values_ref, hi_ref, lo_ref, dense, staged, index_ref, sems,
                 index_sem):
    n = dense.shape[0]
    per = nb // CHUNKS

    def chunk(i):
        part = pl.ds(i * per, per)
        return pltpu.make_async_copy(values_ref.at[part], staged.at[part], sems.at[i])

    index_copy = pltpu.make_async_copy(index_any, index_ref, index_sem)
    index_copy.start()
    for i in range(CHUNKS):
        chunk(i).start()

    @pl.loop(0, n)
    def _(d):
        dense[d] = jnp.zeros(dense.shape[1:], jnp.float32)

    index_copy.wait()

    for i in range(CHUNKS):
        chunk(i).wait()

        @pl.loop(i * per, (i + 1) * per, unroll=4)
        def _(s):
            index = index_ref[s]
            place = index >> 3
            rows = pl.ds(pl.multiple_of((index >> 2 & 1) * bs, bs), bs)
            columns = pl.ds(pl.multiple_of((index >> 1 & 1) * bs, bs), bs)
            live = (index & 1).astype(jnp.float32)
            dense[place, rows, columns] += staged[s].astype(jnp.float32) * live

    @pl.loop(0, n)
    def _(d):
        whole = dense[d]
        head = whole.astype(jnp.bfloat16)
        hi_ref[d] = head
        lo_ref[d] = (whole - head.astype(jnp.float32)).astype(jnp.bfloat16)


def layer_kernel(n, cuts, hi_ref, lo_ref, x_ref, gain_ref, w_ref, out_ref,
                 pa_send, pa_recv, yb_send, yb_recv, zb_send, zb_recv, acc, agg, hbuf, out_t,
                 pa_ss, pa_rs, yb_ss, yb_rs, zb_ss, zb_rs, hz_ss, hz_rs, hy_ss, hy_rs, hc_ss, hc_rs):
    zs = n // 4
    me = lax.axis_index("col")
    z, y, c = me // 4, me // 2 % 2, me % 2
    other_core = me + 1 - 2 * c
    other_y = me + 2 - 4 * y

    def dest(z_to):
        return z_to * 4 + y * 2 + c

    barrier = pltpu.get_barrier_semaphore()

    def greet(device):
        pl.semaphore_signal(barrier, inc=1, device_id={"col": device},
                            device_id_type=pl.DeviceIdType.MESH)

    greet(other_core)
    greet(other_y)
    for i in range(1, zs):
        greet(dest((z + i) % zs))

    def remote(src, dst, ss, rs, device):
        return pltpu.make_async_remote_copy(
            src_ref=src, dst_ref=dst, send_sem=ss, recv_sem=rs,
            device_id={"col": device}, device_id_type=pl.DeviceIdType.MESH)

    def product(place):
        x = x_ref[...]
        return (jnp.dot(hi_ref[place], x, preferred_element_type=jnp.float32)
                + jnp.dot(lo_ref[place], x, preferred_element_type=jnp.float32))

    def core_copy(j):
        return remote(pa_send.at[j], pa_recv.at[j], pa_ss.at[j], pa_rs.at[j], other_core)

    @pl.loop(0, zs)
    def _(k):
        j = (1 - y) * zs + (z + 1 + k) % zs
        pa_send[j] = product((1 - c) * 2 * zs + j)

    pl.semaphore_wait(barrier, zs + 1)

    @pl.loop(0, zs)
    def _(k):
        core_copy((1 - y) * zs + (z + 1 + k) % zs).start()

    half = acc.shape[1] // 2
    halves = (pl.ds(0, half), pl.ds(half, half))

    def y_copy(k, h):
        return remote(yb_send.at[k, halves[h]], yb_recv.at[k, halves[h]],
                      yb_ss.at[2 * k + h], yb_rs.at[2 * k + h], other_y)

    @pl.loop(0, zs)
    def _(k):
        k = (z + 1 + k) % zs
        j = (1 - y) * zs + k
        acc[j] = product(c * 2 * zs + j)
        core_copy(j).wait_recv()
        for h in (0, 1):
            yb_send[k, halves[h]] = (acc[j, halves[h]] + pa_recv[j, halves[h]]).astype(jnp.bfloat16)
            y_copy(k, h).start()

    @pl.loop(0, zs)
    def _(k):
        j = y * zs + (z + 1 + k) % zs
        pa_send[j] = product((1 - c) * 2 * zs + j)
        core_copy(j).start()

    @pl.loop(0, zs)
    def _(k):
        j = y * zs + (z + 1 + k) % zs
        acc[j] = product(c * 2 * zs + j)
        core_copy(j).wait_recv()
        acc[j] = acc[j] + pa_recv[j]

    def z_copy(i, h):
        return remote(zb_send.at[i, halves[h]], zb_recv.at[i, halves[h]],
                      zb_ss.at[2 * i + h], zb_rs.at[2 * i + h], dest((z + i) % zs))

    @pl.loop(1, zs)
    def _(i):
        k = (z + i) % zs
        for h in (0, 1):
            y_copy(k, h).wait_recv()
            zb_send[i, halves[h]] = (
                acc[y * zs + k, halves[h]] + yb_recv[k, halves[h]].astype(jnp.float32)
            ).astype(jnp.bfloat16)
            z_copy(i, h).start()

    for h in (0, 1):
        y_copy(z, h).wait_recv()
    agg[...] = acc[y * zs + z] + yb_recv[z].astype(jnp.float32)

    @pl.loop(1, zs)
    def _(i):
        for h in (0, 1):
            z_copy(i, h).wait_recv()
        agg[...] += zb_recv[i].astype(jnp.float32)

    total = agg[...]
    scale = lax.rsqrt(jnp.mean(total * total, axis=1, keepdims=True) + 1e-06)
    normed = (total * scale * gain_ref[...]).astype(jnp.bfloat16)
    hidden = jnp.maximum(jnp.dot(normed, w_ref[...], preferred_element_type=jnp.float32), 0.0)
    mine = (c * 2 + y) * zs + z
    hbuf[mine] = hidden.T.astype(jnp.bfloat16)

    last = len(cuts) - 1
    pieces = [pl.ds(sum(cuts[:i]), cuts[i]) for i in range(len(cuts))]
    streams = [(p, y) for p in range(len(cuts))] + [(last, 1 - y)]

    def slot_of(c_of, y_of, z_of):
        return (c_of * 2 + y_of) * zs + z_of

    def chain(stream, z_of, way):
        piece, y_of = streams[stream]
        ref = hbuf.at[slot_of(c, y_of, z_of), pieces[piece]]
        return remote(ref, ref, hz_ss.at[(way * len(streams) + stream) * zs + z_of],
                      hz_rs.at[stream * zs + z_of], dest((z + 1 - 2 * way + zs) % zs))

    def across(piece, y_of, z_of):
        ref = hbuf.at[slot_of(c, y_of, z_of), pieces[piece]]
        k = piece * zs + z_of if piece < last else last * zs
        return remote(ref, ref, hy_ss.at[k], hy_rs.at[k], other_y)

    def pair(piece, c_of, y_of, z_of):
        ref = hbuf.at[slot_of(c_of, y_of, z_of), pieces[piece]]
        k = (piece * 2 + y_of) * zs + z_of
        return remote(ref, ref, hc_ss.at[k], hc_rs.at[k], other_core)

    def take(slot):
        out_t[...] += (jnp.dot(hbuf[slot], hi_ref[slot], preferred_element_type=jnp.float32)
                       + jnp.dot(hbuf[slot], lo_ref[slot], preferred_element_type=jnp.float32))

    def can_go(way):
        return z + 1 < zs if way == 0 else z > 0

    def both_ways(i, first, end, do):
        for way in (0, 1):
            z_of = z - i if way == 0 else z + i
            there = (z_of >= 0) if way == 0 else (z_of < zs) & (i > 0)

            @pl.when(there & (i >= first) & (i < end))
            def _():
                do(way, z_of)

    def go_on(stream, z_of, way):
        @pl.when(can_go(way))
        def _():
            chain(stream, z_of, way).start()

    across(last, y, z).start()
    for p in range(len(cuts)):
        for way in (0, 1):
            go_on(p, z, way)
        if p < last:
            across(p, y, z).start()
    for p in range(len(cuts)):
        pair(p, c, y, z).start()
    out_t[...] = jnp.zeros(out_t.shape, jnp.float32)
    take(mine)
    across(last, 1 - y, z).wait_recv()
    for way in (0, 1):
        go_on(len(cuts), z, way)
    pair(last, c, 1 - y, z).start()

    @pl.loop(1, zs + 2)
    def _(i):
        for stream in range(len(streams)):
            def arrive(way, z_of):
                chain(stream, z_of, way).wait_recv()
                go_on(stream, z_of, way)
                piece, y_of = streams[stream]
                if piece < last:
                    across(piece, y, z_of).start()
                pair(piece, c, y_of, z_of).start()

            both_ways(i, 1, zs, arrive)

        both_ways(i, 1, zs, lambda way, z_of: take(slot_of(c, y, z_of)))

        def far(way, z_of):
            for p in range(last):
                across(p, 1 - y, z_of).wait_recv()
                pair(p, c, 1 - y, z_of).start()
            take(slot_of(c, 1 - y, z_of))

        both_ways(i - 1, 0, zs, far)

        def other(way, z_of):
            for y_of in (y, 1 - y):
                for p in range(len(cuts)):
                    pair(p, 1 - c, y_of, z_of).wait_recv()
                take(slot_of(1 - c, y_of, z_of))

        both_ways(i - 2, 0, zs, other)

    out_ref[...] = out_t[...]

    @pl.loop(0, 2 * zs)
    def _(j):
        core_copy(j).wait_send()

    @pl.loop(0, zs)
    def _(k):
        for h in (0, 1):
            y_copy(k, h).wait_send()

    @pl.loop(1, zs)
    def _(i):
        for h in (0, 1):
            z_copy(i, h).wait_send()

    across(last, y, z).wait_send()

    @pl.loop(0, zs)
    def _(k):
        for p in range(len(cuts)):
            if p < last:
                across(p, y, k).wait_send()
            for y_of in (0, 1):
                pair(p, c, y_of, k).wait_send()
        for way in (0, 1):
            from_there = k <= z if way == 0 else k >= z

            @pl.when(can_go(way) & from_there)
            def _():
                for stream in range(len(streams)):
                    chain(stream, k, way).wait_send()


def solution(mesh):
    n = mesh.shape["col"]
    zs = n // 4

    def body(features, block_values, block_owner, block_sub, block_col, block_valid, norm_gain,
             weight):
        nb, bs = block_values.shape[:2]
        rows, width = features.shape
        anywhere = pl.BlockSpec(memory_space=pl.ANY)
        vmem_limit = (n + 6) * 7 // 8 * MIB
        vmem = pl.BlockSpec(memory_space=pltpu.VMEM)
        owner = block_owner[:, 0]
        place = (owner % 2 * 2 + owner // 2 % 2) * zs + owner // 4
        index = ((place * 2 + block_sub) * 2 + block_col) * 2 + block_valid
        blocks = jax.ShapeDtypeStruct((n, rows, rows), jnp.bfloat16)
        hi, lo = pl.pallas_call(
            functools.partial(merge_kernel, bs, nb),
            out_shape=(blocks, blocks),
            in_specs=[anywhere] * 2,
            out_specs=(vmem, vmem),
            scratch_shapes=[
                pltpu.VMEM((n, rows, rows), jnp.float32),
                pltpu.VMEM((nb, bs, bs), jnp.bfloat16),
                pltpu.SMEM((nb,), jnp.int32),
                pltpu.SemaphoreType.DMA((CHUNKS,)),
                pltpu.SemaphoreType.DMA,
            ],
            compiler_params=pltpu.CompilerParams(vmem_limit_bytes=vmem_limit),
        )(index, block_values)

        f32, bf16 = jnp.float32, jnp.bfloat16
        cuts = tuple(width // 16 * part for part in CUTS)
        count = len(cuts)
        dma = pltpu.SemaphoreType.DMA
        return pl.pallas_call(
            functools.partial(layer_kernel, n, cuts),
            out_shape=jax.ShapeDtypeStruct((width, rows), f32),
            in_specs=[vmem] * 5,
            out_specs=vmem,
            scratch_shapes=[
                pltpu.VMEM((2 * zs, rows, width), f32),
                pltpu.VMEM((2 * zs, rows, width), f32),
                pltpu.VMEM((zs, rows, width), bf16),
                pltpu.VMEM((zs, rows, width), bf16),
                pltpu.VMEM((zs, rows, width), bf16),
                pltpu.VMEM((zs, rows, width), bf16),
                pltpu.VMEM((2 * zs, rows, width), f32),
                pltpu.VMEM((rows, width), f32),
                pltpu.VMEM((n, width, rows), bf16),
                pltpu.VMEM((width, rows), f32),
                dma((2 * zs,)), dma((2 * zs,)), dma((2 * zs,)), dma((2 * zs,)), dma((2 * zs,)),
                dma((2 * zs,)),
                dma((2 * (count + 1) * zs,)), dma(((count + 1) * zs,)),
                dma(((count - 1) * zs + 1,)), dma(((count - 1) * zs + 1,)),
                dma((2 * count * zs,)), dma((2 * count * zs,)),
            ],
            compiler_params=pltpu.CompilerParams(
                collective_id=0, has_side_effects=True, vmem_limit_bytes=vmem_limit),
        )(hi, lo, features, norm_gain[None, :], weight).T

    placed = (
        P(("groups", "col"), None),
        P(("groups", "col"), None, None),
        P(("groups", "col"), None),
        P(("groups", "col")),
        P(("groups", "col")),
        P(("groups", "col")),
        P(),
        P(),
    )
    return jax.shard_map(
        body, mesh=mesh, in_specs=placed, out_specs=P(("groups", "col"), None), check_vma=False
    )
```

```python
import functools

import jax
import jax.numpy as jnp
from jax import lax
from jax.experimental import pallas as pl
from jax.experimental.pallas import tpu as pltpu
from jax.sharding import PartitionSpec as P

MIB = 1024 * 1024
CHUNKS = 8
CUTS = (7, 6, 3)


def merge_kernel(bs, nb, index_any, values_ref, hi_ref, lo_ref, dense, staged, index_ref, sems,
                 index_sem):
    n = dense.shape[0]
    per = nb // CHUNKS

    def chunk(i):
        part = pl.ds(i * per, per)
        return pltpu.make_async_copy(values_ref.at[part], staged.at[part], sems.at[i])

    index_copy = pltpu.make_async_copy(index_any, index_ref, index_sem)
    index_copy.start()
    for i in range(CHUNKS):
        chunk(i).start()

    @pl.loop(0, n)
    def _(d):
        dense[d] = jnp.zeros(dense.shape[1:], jnp.float32)

    index_copy.wait()

    for i in range(CHUNKS):
        chunk(i).wait()

        @pl.loop(i * per, (i + 1) * per, unroll=8)
        def _(s):
            index = index_ref[s]
            place = index >> 3
            rows = pl.ds(pl.multiple_of((index >> 2 & 1) * bs, bs), bs)
            columns = pl.ds(pl.multiple_of((index >> 1 & 1) * bs, bs), bs)
            live = (index & 1).astype(jnp.float32)
            dense[place, rows, columns] += staged[s].astype(jnp.float32) * live

    @pl.loop(0, n)
    def _(d):
        whole = dense[d]
        head = whole.astype(jnp.bfloat16)
        hi_ref[d] = head
        lo_ref[d] = (whole - head.astype(jnp.float32)).astype(jnp.bfloat16)


def layer_kernel(n, cuts, hi_ref, lo_ref, x_ref, gain_ref, w_ref, out_ref,
                 pa_send, pa_recv, yb_send, yb_recv, zb_send, zb_recv, acc, agg, hbuf, out_t,
                 pa_ss, pa_rs, yb_ss, yb_rs, zb_ss, zb_rs, hz_ss, hz_rs, hy_ss, hy_rs, hc_ss, hc_rs):
    zs = n // 4
    me = lax.axis_index("col")
    z, y, c = me // 4, me // 2 % 2, me % 2
    other_core = me + 1 - 2 * c
    other_y = me + 2 - 4 * y

    def dest(z_to):
        return z_to * 4 + y * 2 + c

    barrier = pltpu.get_barrier_semaphore()

    def greet(device):
        pl.semaphore_signal(barrier, inc=1, device_id={"col": device},
                            device_id_type=pl.DeviceIdType.MESH)

    greet(other_core)
    greet(other_y)
    for i in range(1, zs):
        greet(dest((z + i) % zs))

    def remote(src, dst, ss, rs, device):
        return pltpu.make_async_remote_copy(
            src_ref=src, dst_ref=dst, send_sem=ss, recv_sem=rs,
            device_id={"col": device}, device_id_type=pl.DeviceIdType.MESH)

    def product(place):
        x = x_ref[...]
        return (jnp.dot(hi_ref[place], x, preferred_element_type=jnp.float32)
                + jnp.dot(lo_ref[place], x, preferred_element_type=jnp.float32))

    def core_copy(j):
        return remote(pa_send.at[j], pa_recv.at[j], pa_ss.at[j], pa_rs.at[j], other_core)

    @pl.loop(0, zs)
    def _(k):
        j = (1 - y) * zs + (z + 1 + k) % zs
        pa_send[j] = product((1 - c) * 2 * zs + j)

    pl.semaphore_wait(barrier, zs + 1)

    @pl.loop(0, zs)
    def _(k):
        core_copy((1 - y) * zs + (z + 1 + k) % zs).start()

    half = acc.shape[1] // 2
    halves = (pl.ds(0, half), pl.ds(half, half))

    def y_copy(k, h):
        return remote(yb_send.at[k, halves[h]], yb_recv.at[k, halves[h]],
                      yb_ss.at[2 * k + h], yb_rs.at[2 * k + h], other_y)

    @pl.loop(0, zs)
    def _(k):
        k = (z + 1 + k) % zs
        j = (1 - y) * zs + k
        acc[j] = product(c * 2 * zs + j)
        core_copy(j).wait_recv()
        for h in (0, 1):
            yb_send[k, halves[h]] = (acc[j, halves[h]] + pa_recv[j, halves[h]]).astype(jnp.bfloat16)
            y_copy(k, h).start()

    @pl.loop(0, zs)
    def _(k):
        j = y * zs + (z + 1 + k) % zs
        pa_send[j] = product((1 - c) * 2 * zs + j)
        core_copy(j).start()

    @pl.loop(0, zs)
    def _(k):
        j = y * zs + (z + 1 + k) % zs
        acc[j] = product(c * 2 * zs + j)
        core_copy(j).wait_recv()
        acc[j] = acc[j] + pa_recv[j]

    def z_copy(i, h):
        return remote(zb_send.at[i, halves[h]], zb_recv.at[i, halves[h]],
                      zb_ss.at[2 * i + h], zb_rs.at[2 * i + h], dest((z + i) % zs))

    @pl.loop(1, zs)
    def _(i):
        k = (z + i) % zs
        for h in (0, 1):
            y_copy(k, h).wait_recv()
            zb_send[i, halves[h]] = (
                acc[y * zs + k, halves[h]] + yb_recv[k, halves[h]].astype(jnp.float32)
            ).astype(jnp.bfloat16)
            z_copy(i, h).start()

    for h in (0, 1):
        y_copy(z, h).wait_recv()
    agg[...] = acc[y * zs + z] + yb_recv[z].astype(jnp.float32)

    @pl.loop(1, zs)
    def _(i):
        for h in (0, 1):
            z_copy(i, h).wait_recv()
        agg[...] += zb_recv[i].astype(jnp.float32)

    total = agg[...]
    scale = lax.rsqrt(jnp.mean(total * total, axis=1, keepdims=True) + 1e-06)
    normed = (total * scale * gain_ref[...]).astype(jnp.bfloat16)
    hidden = jnp.maximum(jnp.dot(normed, w_ref[...], preferred_element_type=jnp.float32), 0.0)
    mine = (c * 2 + y) * zs + z
    hbuf[mine] = hidden.T.astype(jnp.bfloat16)

    last = len(cuts) - 1
    pieces = [pl.ds(sum(cuts[:i]), cuts[i]) for i in range(len(cuts))]
    streams = [(p, y) for p in range(len(cuts))] + [(last, 1 - y)]

    def slot_of(c_of, y_of, z_of):
        return (c_of * 2 + y_of) * zs + z_of

    def chain(stream, z_of, way):
        piece, y_of = streams[stream]
        ref = hbuf.at[slot_of(c, y_of, z_of), pieces[piece]]
        return remote(ref, ref, hz_ss.at[(way * len(streams) + stream) * zs + z_of],
                      hz_rs.at[stream * zs + z_of], dest((z + 1 - 2 * way + zs) % zs))

    def across(piece, y_of, z_of):
        ref = hbuf.at[slot_of(c, y_of, z_of), pieces[piece]]
        k = piece * zs + z_of if piece < last else last * zs
        return remote(ref, ref, hy_ss.at[k], hy_rs.at[k], other_y)

    def pair(piece, c_of, y_of, z_of):
        ref = hbuf.at[slot_of(c_of, y_of, z_of), pieces[piece]]
        k = (piece * 2 + y_of) * zs + z_of
        return remote(ref, ref, hc_ss.at[k], hc_rs.at[k], other_core)

    def take(slot):
        out_t[...] += (jnp.dot(hbuf[slot], hi_ref[slot], preferred_element_type=jnp.float32)
                       + jnp.dot(hbuf[slot], lo_ref[slot], preferred_element_type=jnp.float32))

    def can_go(way):
        return z + 1 < zs if way == 0 else z > 0

    def both_ways(i, first, end, do):
        for way in (0, 1):
            z_of = z - i if way == 0 else z + i
            there = (z_of >= 0) if way == 0 else (z_of < zs) & (i > 0)

            @pl.when(there & (i >= first) & (i < end))
            def _():
                do(way, z_of)

    def go_on(stream, z_of, way):
        @pl.when(can_go(way))
        def _():
            chain(stream, z_of, way).start()

    across(last, y, z).start()
    for p in range(len(cuts)):
        for way in (0, 1):
            go_on(p, z, way)
        if p < last:
            across(p, y, z).start()
    for p in range(len(cuts)):
        pair(p, c, y, z).start()
    out_t[...] = jnp.zeros(out_t.shape, jnp.float32)
    take(mine)
    across(last, 1 - y, z).wait_recv()
    for way in (0, 1):
        go_on(len(cuts), z, way)
    pair(last, c, 1 - y, z).start()

    @pl.loop(1, zs + 2)
    def _(i):
        for stream in range(len(streams)):
            def arrive(way, z_of):
                chain(stream, z_of, way).wait_recv()
                go_on(stream, z_of, way)
                piece, y_of = streams[stream]
                if piece < last:
                    across(piece, y, z_of).start()
                pair(piece, c, y_of, z_of).start()

            both_ways(i, 1, zs, arrive)

        both_ways(i, 1, zs, lambda way, z_of: take(slot_of(c, y, z_of)))

        def far(way, z_of):
            for p in range(last):
                across(p, 1 - y, z_of).wait_recv()
                pair(p, c, 1 - y, z_of).start()
            take(slot_of(c, 1 - y, z_of))

        both_ways(i - 1, 0, zs, far)

        def other(way, z_of):
            for y_of in (y, 1 - y):
                for p in range(len(cuts)):
                    pair(p, 1 - c, y_of, z_of).wait_recv()
                take(slot_of(1 - c, y_of, z_of))

        both_ways(i - 2, 0, zs, other)

    out_ref[...] = out_t[...]

    @pl.loop(0, 2 * zs)
    def _(j):
        core_copy(j).wait_send()

    @pl.loop(0, zs)
    def _(k):
        for h in (0, 1):
            y_copy(k, h).wait_send()

    @pl.loop(1, zs)
    def _(i):
        for h in (0, 1):
            z_copy(i, h).wait_send()

    across(last, y, z).wait_send()

    @pl.loop(0, zs)
    def _(k):
        for p in range(len(cuts)):
            if p < last:
                across(p, y, k).wait_send()
            for y_of in (0, 1):
                pair(p, c, y_of, k).wait_send()
        for way in (0, 1):
            from_there = k <= z if way == 0 else k >= z

            @pl.when(can_go(way) & from_there)
            def _():
                for stream in range(len(streams)):
                    chain(stream, k, way).wait_send()


def solution(mesh):
    n = mesh.shape["col"]
    zs = n // 4

    def body(features, block_values, block_owner, block_sub, block_col, block_valid, norm_gain,
             weight):
        nb, bs = block_values.shape[:2]
        rows, width = features.shape
        anywhere = pl.BlockSpec(memory_space=pl.ANY)
        vmem_limit = (n + 6) * 7 // 8 * MIB
        vmem = pl.BlockSpec(memory_space=pltpu.VMEM)
        owner = block_owner[:, 0]
        place = (owner % 2 * 2 + owner // 2 % 2) * zs + owner // 4
        index = ((place * 2 + block_sub) * 2 + block_col) * 2 + block_valid
        blocks = jax.ShapeDtypeStruct((n, rows, rows), jnp.bfloat16)
        hi, lo = pl.pallas_call(
            functools.partial(merge_kernel, bs, nb),
            out_shape=(blocks, blocks),
            in_specs=[anywhere] * 2,
            out_specs=(vmem, vmem),
            scratch_shapes=[
                pltpu.VMEM((n, rows, rows), jnp.float32),
                pltpu.VMEM((nb, bs, bs), jnp.bfloat16),
                pltpu.SMEM((nb,), jnp.int32),
                pltpu.SemaphoreType.DMA((CHUNKS,)),
                pltpu.SemaphoreType.DMA,
            ],
            compiler_params=pltpu.CompilerParams(vmem_limit_bytes=vmem_limit),
        )(index, block_values)

        f32, bf16 = jnp.float32, jnp.bfloat16
        cuts = tuple(width // 16 * part for part in CUTS)
        count = len(cuts)
        dma = pltpu.SemaphoreType.DMA
        return pl.pallas_call(
            functools.partial(layer_kernel, n, cuts),
            out_shape=jax.ShapeDtypeStruct((width, rows), f32),
            in_specs=[vmem] * 5,
            out_specs=vmem,
            scratch_shapes=[
                pltpu.VMEM((2 * zs, rows, width), f32),
                pltpu.VMEM((2 * zs, rows, width), f32),
                pltpu.VMEM((zs, rows, width), bf16),
                pltpu.VMEM((zs, rows, width), bf16),
                pltpu.VMEM((zs, rows, width), bf16),
                pltpu.VMEM((zs, rows, width), bf16),
                pltpu.VMEM((2 * zs, rows, width), f32),
                pltpu.VMEM((rows, width), f32),
                pltpu.VMEM((n, width, rows), bf16),
                pltpu.VMEM((width, rows), f32),
                dma((2 * zs,)), dma((2 * zs,)), dma((2 * zs,)), dma((2 * zs,)), dma((2 * zs,)),
                dma((2 * zs,)),
                dma((2 * (count + 1) * zs,)), dma(((count + 1) * zs,)),
                dma(((count - 1) * zs + 1,)), dma(((count - 1) * zs + 1,)),
                dma((2 * count * zs,)), dma((2 * count * zs,)),
            ],
            compiler_params=pltpu.CompilerParams(
                collective_id=0, has_side_effects=True, vmem_limit_bytes=vmem_limit),
        )(hi, lo, features, norm_gain[None, :], weight).T

    placed = (
        P(("groups", "col"), None),
        P(("groups", "col"), None, None),
        P(("groups", "col"), None),
        P(("groups", "col")),
        P(("groups", "col")),
        P(("groups", "col")),
        P(),
        P(),
    )
    return jax.shard_map(
        body, mesh=mesh, in_specs=placed, out_specs=P(("groups", "col"), None), check_vma=False
    )
```
